32 devices in a mesh: groups: 2 (over x), dp: 8 (over z, y), tensor: 2 (over core).
Axes of the slice: x: 2, y: 2, z: 4, core: 2. Of those that a mesh axis runs over, the one named last changes fastest.
Arguments:
- train_hidden: bfloat16 [32, 256, 14336], P(('groups', 'dp'), None, 'tensor'), parts along dimension 0, may hold values from -6 to 6
- train_outgrad: bfloat16 [32, 256, 4096], P(('groups', 'dp'), None, 'tensor'), parts along dimension 0, may hold values from -6 to 6
- train_padding: int32 [32], P(('groups', 'dp')), parts along dimension 0, may hold values from 0 to 128
- query_hidden: bfloat16 [32, 64, 14336], P(('groups', 'dp'), None, 'tensor'), parts along dimension 0, may hold values from -6 to 6
- query_outgrad: bfloat16 [32, 64, 4096], P(('groups', 'dp'), None, 'tensor'), parts along dimension 0, may hold values from -6 to 6
- query_padding: int32 [32], P(('groups', 'dp')), parts along dimension 0, may hold values from 0 to 32
- proj_in: bfloat16 [64, 14336], P(None, 'tensor'), may hold values from -0.046875 to 0.046875
- output_projection: bfloat16 [64, 4096], P(None, 'tensor'), may hold values from -0.09375 to 0.09375
- in_inverse: float32 [64, 64], replicated, may hold values from -0.2 to 2.2, as said below
- output_inverse: float32 [64, 64], replicated, may hold values from -0.2 to 2.2, as said below
Outputs:
- scores: float32 [32, 16], P(('groups', 'dp')), parts along dimension 0
The draws below stay inside these ranges and needn't reach their ends.
There are 2 independent parts, one for each index of `groups`. The reference program is written for one: setup_inputs(seed, part) draws one part's arguments, and reference() takes and returns one part's arrays. A program takes and returns all parts, laid end to end along the dimension named above; an argument that names none is the same for every part. Nothing has to cross between parts.
Inputs may be any that keep to these rules, and one draw needn't show every extreme that they name: `in_inverse`: a given inverse factor. `output_inverse`: a given inverse factor.
All inputs are finite; a program needn't handle non-finite values.
Results may differ from the reference program's by a relative error of at most 0.0003.
Values sent between devices are 32-bit elements; how exact they have to be, the bound alone decides.
A program may use at most 64 MiB of HBM per device.

```python
import jax
import jax.numpy as jnp
from jax import lax

D = 4096
FF = 14336
K = 64
LEN = 256
QLEN = 64
TRAIN = 16
QUERIES = 16


def inverse_factor(key):
    diag_key, off_key = jax.random.split(key)
    diagonal = jax.random.uniform(diag_key, (K,), jnp.float32, 1.0, 2.0)
    off_part = jnp.clip(0.05 * jax.random.normal(off_key, (K, K), jnp.float32), -0.2, 0.2)
    identity = jnp.eye(K, dtype=jnp.float32)
    return identity * diagonal[None, :] + off_part * (1.0 - identity)


def draw_in_inverse(key, part):
    key = jax.random.fold_in(key, 11)
    return inverse_factor(key)


def draw_output_inverse(key, part):
    key = jax.random.fold_in(key, 23)
    return inverse_factor(key)


def with_ends(array, own_key, least, largest):
    longest = array.shape.index(max(array.shape))
    spots = []
    for shift in (0, 1):
        where = [jax.random.randint(jax.random.fold_in(own_key, axis), (), 0, length) for axis, length in enumerate(array.shape)]
        where[longest] = (where[longest] + shift) % array.shape[longest]
        spots.append(tuple(where))
    return array.at[spots[0]].set(least).at[spots[1]].set(largest)


def block_scale(own_key, dims, cuts, low, top_value):
    factor_of = 1.0
    for position, shards_of in cuts:
        heights = jax.random.uniform(jax.random.fold_in(jax.random.fold_in(own_key, 6), position), (shards_of,), jnp.float32, low / len(cuts), top_value / len(cuts))
        factor_of = factor_of * jnp.repeat(jnp.exp(heights), dims[position] // shards_of).reshape((-1,) + (1,) * (len(dims) - 1 - position))
    return factor_of


def scatter_about(own_key, shape, scale, reach, pieces=(), kind=jnp.bfloat16):
    array = scale * jax.random.normal(own_key, shape, jnp.float32)
    if pieces:
        array = array * block_scale(own_key, shape, pieces, -0.22, 0.18)
    return jnp.clip(array, -reach, reach).astype(kind)


def setup_inputs(seed: int = 0, part: int = 0) -> dict:
    keys = jax.random.split(jax.random.key(seed), 11)
    part_splits = jax.random.split(jax.random.fold_in(keys[10], part), 11)
    return {
        "train_hidden": scatter_about(part_splits[0], (TRAIN, LEN, FF), 1.0, 6.0, ((0, 8), (2, 2))),
        "train_outgrad": scatter_about(part_splits[1], (TRAIN, LEN, D), 1.0, 6.0, ((0, 8), (2, 2))),
        "train_padding": with_ends(jax.random.randint(part_splits[2], (TRAIN,), 0, LEN // 2 + 1), jax.random.fold_in(part_splits[2], 1), 0, (LEN // 2 + 1) - 1).astype(jnp.int32),
        "query_hidden": scatter_about(part_splits[3], (QUERIES, QLEN, FF), 1.0, 6.0, ((0, 8), (2, 2))),
        "query_outgrad": scatter_about(part_splits[4], (QUERIES, QLEN, D), 1.0, 6.0, ((0, 8), (2, 2))),
        "query_padding": with_ends(jax.random.randint(part_splits[5], (QUERIES,), 0, QLEN // 2 + 1), jax.random.fold_in(part_splits[5], 1), 0, (QLEN // 2 + 1) - 1).astype(jnp.int32),
        "proj_in": scatter_about(keys[6], (K, FF), FF ** -0.5, 0.046875, ((1, 2),)),
        "output_projection": scatter_about(keys[7], (K, D), D ** -0.5, 0.09375, ((1, 2),)),
        "in_inverse": draw_in_inverse(jax.random.fold_in(keys[10], 71), part),
        "output_inverse": draw_output_inverse(jax.random.fold_in(keys[10], 71), part),
    }


HIGH = lax.Precision.HIGHEST


def make_blocks(hidden, output_gradient, padding_mask, proj_in, output_projection):
    length = hidden.shape[1]
    proj_in32 = proj_in.astype(jnp.float32)
    proj_out32 = output_projection.astype(jnp.float32)

    def one_sequence(items):
        seq_hidden, seq_grad, seq_pad = items
        in_side = jnp.dot(proj_in32, seq_hidden.astype(jnp.float32).T, precision=HIGH)
        output_facing = jnp.dot(proj_out32, seq_grad.astype(jnp.float32).T, precision=HIGH)
        positions = jnp.arange(length, dtype=jnp.int32)
        validity = (positions < (length - seq_pad)).astype(jnp.float32)
        counted_tokens = (length - seq_pad).astype(jnp.float32)
        weighted = output_facing * (validity / counted_tokens)[None, :]
        return jnp.dot(weighted, in_side.T, precision=HIGH)

    return lax.map(one_sequence, (hidden, output_gradient, padding_mask))


def reference(train_hidden, train_outgrad, train_padding, query_hidden, query_outgrad, query_padding, proj_in, output_projection, in_inverse, output_inverse):
    train_blocks = make_blocks(train_hidden, train_outgrad, train_padding, proj_in, output_projection)
    query_blocks = make_blocks(query_hidden, query_outgrad, query_padding, proj_in, output_projection)
    left = jnp.einsum('ij,qjk->qik', output_inverse, query_blocks, precision=HIGH)
    conditioned_factor = jnp.einsum('qik,kl->qil', left, in_inverse, precision=HIGH)
    train_flat = train_blocks.reshape(train_blocks.shape[0], -1)
    query_flat = conditioned_factor.reshape(conditioned_factor.shape[0], -1)
    return jnp.dot(train_flat, query_flat.T, precision=HIGH)
```

```python
import functools

import jax
import jax.numpy as jnp
from jax import lax
from jax.experimental import pallas as pl
from jax.experimental.pallas import tpu as pltpu
from jax.sharding import PartitionSpec as P

F32 = jnp.float32
BF16 = jnp.bfloat16
NT = (((1,), (1,)), ((), ()))
TN = (((0,), (0,)), ((), ()))
NN = (((1,), (0,)), ((), ()))


def dot(a, b, dims):
    return lax.dot_general(a, b, dims, preferred_element_type=F32)


def halves(x):
    high = x.astype(BF16)
    return high, (x - high.astype(F32)).astype(BF16)


def dot32(a, b, dims):
    a_high, a_low = halves(a)
    b_high, b_low = halves(b)
    return dot(a_high, b_high, dims) + (dot(a_high, b_low, dims) + dot(a_low, b_high, dims))


def outer(out_side, in_side):
    width = out_side.shape[1]
    left = jnp.concatenate(halves(out_side), axis=1)
    right = jnp.concatenate(halves(in_side), axis=1)
    full = dot(left, right, TN)
    return full[:width, :width] + (full[:width, width:] + full[width:, :width])


def pack(x):
    half = x.shape[0] // 2
    return jnp.concatenate([x[:half], x[half:]], axis=1)


def unpack(x):
    half = x.shape[1] // 2
    return jnp.concatenate([x[:, :half], x[:, half:]], axis=0)


def token_weights(tokens, first, length, padding):
    position = first + lax.broadcasted_iota(jnp.int32, (tokens, 1), 0)
    count = jnp.full((tokens, 1), length - padding, jnp.int32)
    return jnp.where(position < count, 1.0 / count.astype(F32), 0.0)


def kernel(
    n,
    chunk,
    th, tg, tp, qh, qg, qp, pi, po, ii, oi,
    out,
    th_v, tg_v, tp_s, qh_v, qg_v, qp_s, pi_v, po_v, ii_v, oi_v,
    q_mine, q_send, q_recv,
    o_send, o_recv, i_send, i_recv, gathered,
    load_sem, h_sem, ex_send, ex_recv, o_ssem, o_rsem, i_ssem, i_rsem,
    g_ssem, g_rsem, f_ssem, f_rsem,
):
    seqs, length, _ = th.shape
    queries, q_length, _ = qh.shape
    chunks = length // chunk
    me = lax.axis_index("dp")
    core = lax.axis_index("tensor")
    other = 1 - core

    def load(src, dst, k):
        copy = pltpu.make_async_copy(src, dst, load_sem.at[k])
        copy.start()
        return copy

    load_po = load(po, po_v, 0)
    load_qg = load(qg, qg_v, 1)
    load_pi = load(pi, pi_v, 2)
    load_qh = load(qh, qh_v, 3)
    load_qp = load(qp, qp_s, 4)
    load_tp = load(tp, tp_s, 5)
    load_oi = load(oi, oi_v, 6)
    load_ii = load(ii, ii_v, 7)
    load_tg = load(tg, tg_v, 8)
    load_th = []
    for s in range(seqs):
        for j in range(chunks):
            rows = pl.ds(j * chunk, chunk)
            copy = pltpu.make_async_copy(th.at[s, rows], th_v.at[s, rows], h_sem.at[s, j])
            copy.start()
            load_th.append(copy)

    barrier = pltpu.get_barrier_semaphore()
    for k in range(1, n):
        pl.semaphore_signal(barrier, inc=1, device_id={"dp": lax.rem(me + k, n)})
    pl.semaphore_signal(barrier, inc=1, device_id={"tensor": other})

    pending = []

    def send(src, dst, ssem, rsem, where):
        copy = pltpu.make_async_remote_copy(
            src_ref=src, dst_ref=dst, send_sem=ssem, recv_sem=rsem, device_id=where
        )
        copy.start()
        pending.append(copy)
        return copy

    load_po.wait()
    load_qg.wait()
    q_out = dot(qg_v[...].reshape(queries * q_length, -1), po_v[...], NT)
    load_pi.wait()
    load_qh.wait()
    q_in = dot(qh_v[...].reshape(queries * q_length, -1), pi_v[...], NT)
    q_both = jnp.concatenate([q_in, q_out], axis=1)
    first, second = q_both[:q_length], q_both[q_length:]
    q_send[...] = jnp.where(core == 0, second, first)
    q_mine[...] = jnp.where(core == 0, first, second)
    pl.semaphore_wait(barrier, n)
    ex_q = send(q_send, q_recv, ex_send, ex_recv, {"tensor": other})

    load_tg.wait()
    ex_o = []
    for s in range(seqs):
        o_send[s] = pack(dot(tg_v[s], po_v[...], NT))
        ex_o.append(send(o_send.at[s], o_recv.at[s], o_ssem.at[s], o_rsem.at[s], {"tensor": other}))

    width = pi.shape[0]
    load_qp.wait()
    load_oi.wait()
    load_ii.wait()
    ex_q.wait_recv()
    total = q_mine[...] + q_recv[...]
    padding = jnp.where(core == 0, qp_s[0], qp_s[1])
    weights = token_weights(q_length, 0, q_length, padding)
    block = outer(total[:, width:] * weights, total[:, :width])
    conditioned = dot32(dot32(oi_v[...], block, NN), ii_v[...], NN)
    slot = me * queries + core
    gathered[slot] = pack(conditioned)
    ex_g = []
    for k in range(1, n):
        ex_g.append(
            send(gathered.at[slot], gathered.at[slot], g_ssem.at[k], g_rsem.at[k], {"dp": lax.rem(me + k, n)})
        )
    ex_f = [send(gathered.at[slot], gathered.at[slot], f_ssem.at[0], f_rsem.at[0], {"tensor": other})]

    def pass_on(k):
        ex_g[k - 1].wait_recv()
        source = lax.rem(me + (n - k), n) * queries + core
        ex_f.append(
            send(gathered.at[source], gathered.at[source], f_ssem.at[k], f_rsem.at[k], {"tensor": other})
        )

    ex_i = []
    for s in range(seqs):
        for j in range(chunks):
            load_th[s * chunks + j].wait()
            i_send[s, j] = pack(dot(th_v[s, pl.ds(j * chunk, chunk), :], pi_v[...], NT))
            ex_i.append(
                send(i_send.at[s, j], i_recv.at[s, j], i_ssem.at[s, j], i_rsem.at[s, j], {"tensor": other})
            )
    for k in range(1, n):
        pass_on(k)

    load_tp.wait()
    facing = []
    for s in range(seqs):
        ex_o[s].wait_recv()
        weights = token_weights(length, 0, length, tp_s[s])
        facing.append(unpack(o_send[s] + o_recv[s]) * weights)

    ones = jnp.ones((8, 2 * width), BF16)
    for s in range(seqs):
        block = jnp.zeros((width, width), F32)
        for j in range(chunks):
            ex_i[s * chunks + j].wait_recv()
            in_side = unpack(i_send[s, j] + i_recv[s, j])
            block += outer(facing[s][j * chunk : (j + 1) * chunk], in_side)
        if s == 0:
            for copy in ex_f:
                copy.wait_recv()
        sums = jnp.sum(gathered[...] * pack(block)[None], axis=1)
        high, low = halves(sums)
        out[pl.ds(s, 1), :] = (dot(ones, high, NT) + dot(ones, low, NT))[:1]

    for copy in pending:
        copy.wait_send()


def on_device(n, th, tg, tp, qh, qg, qp, pi, po, ii, oi):
    seqs, length, ff = th.shape
    queries, q_length, _ = qh.shape
    width = pi.shape[0]
    chunk = 128
    chunks = length // chunk
    dma = pltpu.SemaphoreType.DMA
    hbm = pl.BlockSpec(memory_space=pl.ANY)
    return pl.pallas_call(
        functools.partial(kernel, n, chunk),
        out_shape=jax.ShapeDtypeStruct((seqs, n * queries), F32),
        in_specs=[hbm] * 10,
        out_specs=pl.BlockSpec(memory_space=pltpu.VMEM),
        scratch_shapes=[
            pltpu.VMEM(th.shape, BF16),
            pltpu.VMEM(tg.shape, BF16),
            pltpu.SMEM(tp.shape, jnp.int32),
            pltpu.VMEM(qh.shape, BF16),
            pltpu.VMEM(qg.shape, BF16),
            pltpu.SMEM(qp.shape, jnp.int32),
            pltpu.VMEM(pi.shape, BF16),
            pltpu.VMEM(po.shape, BF16),
            pltpu.VMEM(ii.shape, F32),
            pltpu.VMEM(oi.shape, F32),
            pltpu.VMEM((q_length, 2 * width), F32),
            pltpu.VMEM((q_length, 2 * width), F32),
            pltpu.VMEM((q_length, 2 * width), F32),
            pltpu.VMEM((seqs, length // 2, 2 * width), F32),
            pltpu.VMEM((seqs, length // 2, 2 * width), F32),
            pltpu.VMEM((seqs, chunks, chunk // 2, 2 * width), F32),
            pltpu.VMEM((seqs, chunks, chunk // 2, 2 * width), F32),
            pltpu.VMEM((n * queries, width // 2, 2 * width), F32),
            dma((9,)),
            dma((seqs, chunks)),
            dma,
            dma,
            dma((seqs,)),
            dma((seqs,)),
            dma((seqs, chunks)),
            dma((seqs, chunks)),
            dma((n,)),
            dma((n,)),
            dma((n,)),
            dma((n,)),
        ],
        compiler_params=pltpu.CompilerParams(
            collective_id=0, has_side_effects=True, vmem_limit_bytes=56 * 1024 * 1024
        ),
        cost_estimate=pl.CostEstimate(
            flops=2 * width * (seqs * length + queries * q_length) * (ff + tg.shape[2]),
            bytes_accessed=2 * (seqs * length + queries * q_length) * (ff + tg.shape[2]),
            transcendentals=0,
        ),
    )(th, tg, tp, qh, qg, qp, pi, po, ii, oi)


def solution(mesh):
    rows = ("groups", "dp")
    in_specs = (
        P(rows, None, "tensor"),
        P(rows, None, "tensor"),
        P(rows),
        P(rows, None, "tensor"),
        P(rows, None, "tensor"),
        P(rows),
        P(None, "tensor"),
        P(None, "tensor"),
        P(),
        P(),
    )
    return jax.shard_map(
        functools.partial(on_device, mesh.shape["dp"]),
        mesh=mesh,
        in_specs=in_specs,
        out_specs=P(rows, None),
        check_vma=False,
    )
```

```python
import functools

import jax
import jax.numpy as jnp
from jax import lax
from jax.experimental import pallas as pl
from jax.experimental.pallas import tpu as pltpu
from jax.sharding import PartitionSpec as P

F32 = jnp.float32
BF16 = jnp.bfloat16
NT = (((1,), (1,)), ((), ()))
TN = (((0,), (0,)), ((), ()))
NN = (((1,), (0,)), ((), ()))


def dot(a, b, dims):
    return lax.dot_general(a, b, dims, preferred_element_type=F32)


def halves(x):
    high = x.astype(BF16)
    return high, (x - high.astype(F32)).astype(BF16)


def dot32(a, b, dims):
    a_high, a_low = halves(a)
    b_high, b_low = halves(b)
    return dot(a_high, b_high, dims) + (dot(a_high, b_low, dims) + dot(a_low, b_high, dims))


def outer(out_side, in_side):
    width = out_side.shape[1]
    left = jnp.concatenate(halves(out_side), axis=1)
    right = jnp.concatenate(halves(in_side), axis=1)
    full = dot(left, right, TN)
    return full[:width, :width] + (full[:width, width:] + full[width:, :width])


def pack(x):
    half = x.shape[0] // 2
    return jnp.concatenate([x[:half], x[half:]], axis=1)


def unpack(x):
    half = x.shape[1] // 2
    return jnp.concatenate([x[:, :half], x[:, half:]], axis=0)


def token_weights(tokens, first, length, padding):
    position = first + lax.broadcasted_iota(jnp.int32, (tokens, 1), 0)
    count = jnp.full((tokens, 1), length - padding, jnp.int32)
    return jnp.where(position < count, 1.0 / count.astype(F32), 0.0)


def kernel(
    n,
    chunk,
    th, tg, tp, qh, qg, qp, pi, po, ii, oi,
    out,
    th_v, tg_v, tp_s, qh_v, qg_v, qp_s, pi_v, po_v, ii_v, oi_v,
    q_mine, q_send, q_recv,
    o_send, o_recv, i_send, i_recv, gathered,
    load_sem, h_sem, ex_send, ex_recv, o_ssem, o_rsem, i_ssem, i_rsem,
    g_ssem, g_rsem, f_ssem, f_rsem,
):
    seqs, length, _ = th.shape
    queries, q_length, _ = qh.shape
    chunks = length // chunk
    me = lax.axis_index("dp")
    core = lax.axis_index("tensor")
    other = 1 - core

    def load(src, dst, k):
        copy = pltpu.make_async_copy(src, dst, load_sem.at[k])
        copy.start()
        return copy

    load_po = load(po, po_v, 0)
    load_qg = load(qg, qg_v, 1)
    load_pi = load(pi, pi_v, 2)
    load_qh = load(qh, qh_v, 3)
    load_qp = load(qp, qp_s, 4)
    load_tp = load(tp, tp_s, 5)
    load_oi = load(oi, oi_v, 6)
    load_ii = load(ii, ii_v, 7)
    barrier = pltpu.get_barrier_semaphore()
    for k in range(1, n):
        pl.semaphore_signal(barrier, inc=1, device_id={"dp": lax.rem(me + k, n)})
    pl.semaphore_signal(barrier, inc=1, device_id={"tensor": other})

    pending = []

    def send(src, dst, ssem, rsem, where):
        copy = pltpu.make_async_remote_copy(
            src_ref=src, dst_ref=dst, send_sem=ssem, recv_sem=rsem, device_id=where
        )
        copy.start()
        pending.append(copy)
        return copy

    load_po.wait()
    load_qg.wait()
    q_out = dot(qg_v[...].reshape(queries * q_length, -1), po_v[...], NT)
    load_pi.wait()
    load_qh.wait()
    load_tg = load(tg, tg_v, 8)
    load_th = []
    for s in range(seqs):
        for j in range(chunks):
            rows = pl.ds(j * chunk, chunk)
            copy = pltpu.make_async_copy(th.at[s, rows], th_v.at[s, rows], h_sem.at[s, j])
            copy.start()
            load_th.append(copy)

    q_in = dot(qh_v[...].reshape(queries * q_length, -1), pi_v[...], NT)
    q_both = jnp.concatenate([q_in, q_out], axis=1)
    first, second = q_both[:q_length], q_both[q_length:]
    q_send[...] = jnp.where(core == 0, second, first)
    q_mine[...] = jnp.where(core == 0, first, second)
    pl.semaphore_wait(barrier, n)
    ex_q = send(q_send, q_recv, ex_send, ex_recv, {"tensor": other})

    width = pi.shape[0]
    load_qp.wait()
    load_oi.wait()
    load_ii.wait()
    ex_q.wait_recv()
    total = q_mine[...] + q_recv[...]
    padding = jnp.where(core == 0, qp_s[0], qp_s[1])
    weights = token_weights(q_length, 0, q_length, padding)
    block = outer(total[:, width:] * weights, total[:, :width])
    conditioned = dot32(dot32(oi_v[...], block, NN), ii_v[...], NN)
    slot = me * queries + core
    gathered[slot] = pack(conditioned)
    ex_g = []
    for k in range(1, n):
        ex_g.append(
            send(gathered.at[slot], gathered.at[slot], g_ssem.at[k], g_rsem.at[k], {"dp": lax.rem(me + k, n)})
        )
    ex_f = [send(gathered.at[slot], gathered.at[slot], f_ssem.at[0], f_rsem.at[0], {"tensor": other})]

    def pass_on(k):
        ex_g[k - 1].wait_recv()
        source = lax.rem(me + (n - k), n) * queries + core
        ex_f.append(
            send(gathered.at[source], gathered.at[source], f_ssem.at[k], f_rsem.at[k], {"tensor": other})
        )

    load_tg.wait()
    ex_o = []
    for s in range(seqs):
        o_send[s] = pack(dot(tg_v[s], po_v[...], NT))
        ex_o.append(send(o_send.at[s], o_recv.at[s], o_ssem.at[s], o_rsem.at[s], {"tensor": other}))

    ex_i = []
    for s in range(seqs):
        for j in range(chunks):
            load_th[s * chunks + j].wait()
            i_send[s, j] = pack(dot(th_v[s, pl.ds(j * chunk, chunk), :], pi_v[...], NT))
            ex_i.append(
                send(i_send.at[s, j], i_recv.at[s, j], i_ssem.at[s, j], i_rsem.at[s, j], {"tensor": other})
            )
    load_tp.wait()
    facing = []
    for s in range(seqs):
        ex_o[s].wait_recv()
        weights = token_weights(length, 0, length, tp_s[s])
        facing.append(unpack(o_send[s] + o_recv[s]) * weights)

    for k in range(1, n):
        pass_on(k)

    ones = jnp.ones((8, 2 * width), BF16)
    for s in range(seqs):
        block = jnp.zeros((width, width), F32)
        for j in range(chunks):
            ex_i[s * chunks + j].wait_recv()
            in_side = unpack(i_send[s, j] + i_recv[s, j])
            block += outer(facing[s][j * chunk : (j + 1) * chunk], in_side)
        if s == 0:
            for copy in ex_f:
                copy.wait_recv()
        sums = jnp.sum(gathered[...] * pack(block)[None], axis=1)
        high, low = halves(sums)
        out[pl.ds(s, 1), :] = (dot(ones, high, NT) + dot(ones, low, NT))[:1]

    for copy in pending:
        copy.wait_send()


def on_device(n, th, tg, tp, qh, qg, qp, pi, po, ii, oi):
    seqs, length, ff = th.shape
    queries, q_length, _ = qh.shape
    width = pi.shape[0]
    chunk = 256
    chunks = length // chunk
    dma = pltpu.SemaphoreType.DMA
    hbm = pl.BlockSpec(memory_space=pl.ANY)
    return pl.pallas_call(
        functools.partial(kernel, n, chunk),
        out_shape=jax.ShapeDtypeStruct((seqs, n * queries), F32),
        in_specs=[hbm] * 10,
        out_specs=pl.BlockSpec(memory_space=pltpu.VMEM),
        scratch_shapes=[
            pltpu.VMEM(th.shape, BF16),
            pltpu.VMEM(tg.shape, BF16),
            pltpu.SMEM(tp.shape, jnp.int32),
            pltpu.VMEM(qh.shape, BF16),
            pltpu.VMEM(qg.shape, BF16),
            pltpu.SMEM(qp.shape, jnp.int32),
            pltpu.VMEM(pi.shape, BF16),
            pltpu.VMEM(po.shape, BF16),
            pltpu.VMEM(ii.shape, F32),
            pltpu.VMEM(oi.shape, F32),
            pltpu.VMEM((q_length, 2 * width), F32),
            pltpu.VMEM((q_length, 2 * width), F32),
            pltpu.VMEM((q_length, 2 * width), F32),
            pltpu.VMEM((seqs, length // 2, 2 * width), F32),
            pltpu.VMEM((seqs, length // 2, 2 * width), F32),
            pltpu.VMEM((seqs, chunks, chunk // 2, 2 * width), F32),
            pltpu.VMEM((seqs, chunks, chunk // 2, 2 * width), F32),
            pltpu.VMEM((n * queries, width // 2, 2 * width), F32),
            dma((9,)),
            dma((seqs, chunks)),
            dma,
            dma,
            dma((seqs,)),
            dma((seqs,)),
            dma((seqs, chunks)),
            dma((seqs, chunks)),
            dma((n,)),
            dma((n,)),
            dma((n,)),
            dma((n,)),
        ],
        compiler_params=pltpu.CompilerParams(
            collective_id=0, has_side_effects=True, vmem_limit_bytes=56 * 1024 * 1024
        ),
        cost_estimate=pl.CostEstimate(
            flops=2 * width * (seqs * length + queries * q_length) * (ff + tg.shape[2]),
            bytes_accessed=2 * (seqs * length + queries * q_length) * (ff + tg.shape[2]),
            transcendentals=0,
        ),
    )(th, tg, tp, qh, qg, qp, pi, po, ii, oi)


def solution(mesh):
    rows = ("groups", "dp")
    in_specs = (
        P(rows, None, "tensor"),
        P(rows, None, "tensor"),
        P(rows),
        P(rows, None, "tensor"),
        P(rows, None, "tensor"),
        P(rows),
        P(None, "tensor"),
        P(None, "tensor"),
        P(),
        P(),
    )
    return jax.shard_map(
        functools.partial(on_device, mesh.shape["dp"]),
        mesh=mesh,
        in_specs=in_specs,
        out_specs=P(rows, None),
        check_vma=False,
    )
```

```python
import functools

import jax
import jax.numpy as jnp
from jax import lax
from jax.experimental import pallas as pl
from jax.experimental.pallas import tpu as pltpu
from jax.sharding import PartitionSpec as P

F32 = jnp.float32
BF16 = jnp.bfloat16
NT = (((1,), (1,)), ((), ()))
TN = (((0,), (0,)), ((), ()))
NN = (((1,), (0,)), ((), ()))


def dot(a, b, dims):
    return lax.dot_general(a, b, dims, preferred_element_type=F32)


def halves(x):
    high = x.astype(BF16)
    return high, (x - high.astype(F32)).astype(BF16)


def dot32(a, b, dims):
    a_high, a_low = halves(a)
    b_high, b_low = halves(b)
    return dot(a_high, b_high, dims) + (dot(a_high, b_low, dims) + dot(a_low, b_high, dims))


def outer(out_side, in_side):
    width = out_side.shape[1]
    left = jnp.concatenate(halves(out_side), axis=1)
    right = jnp.concatenate(halves(in_side), axis=1)
    full = dot(left, right, TN)
    return full[:width, :width] + (full[:width, width:] + full[width:, :width])


def pack(x):
    half = x.shape[0] // 2
    return jnp.concatenate([x[:half], x[half:]], axis=1)


def unpack(x):
    half = x.shape[1] // 2
    return jnp.concatenate([x[:, :half], x[:, half:]], axis=0)


def token_weights(tokens, first, length, padding):
    position = first + lax.broadcasted_iota(jnp.int32, (tokens, 1), 0)
    count = jnp.full((tokens, 1), length - padding, jnp.int32)
    return jnp.where(position < count, 1.0 / count.astype(F32), 0.0)


def kernel(
    n,
    chunk,
    th, tg, tp, qh, qg, qp, pi, po, ii, oi,
    out,
    th_v, tg_v, tp_s, qh_v, qg_v, qp_s, pi_v, po_v, ii_v, oi_v,
    q_mine, q_send, q_recv,
    o_send, o_recv, i_send, i_recv, gathered,
    load_sem, h_sem, ex_send, ex_recv, o_ssem, o_rsem, i_ssem, i_rsem,
    g_ssem, g_rsem, f_ssem, f_rsem,
):
    seqs, length, _ = th.shape
    queries, q_length, _ = qh.shape
    chunks = length // chunk
    me = lax.axis_index("dp")
    core = lax.axis_index("tensor")
    other = 1 - core

    def load(src, dst, k):
        copy = pltpu.make_async_copy(src, dst, load_sem.at[k])
        copy.start()
        return copy

    load_po = load(po, po_v, 0)
    load_qg = load(qg, qg_v, 1)
    load_pi = load(pi, pi_v, 2)
    load_qh = load(qh, qh_v, 3)
    load_qp = load(qp, qp_s, 4)
    load_tp = load(tp, tp_s, 5)
    load_oi = load(oi, oi_v, 6)
    load_ii = load(ii, ii_v, 7)
    barrier = pltpu.get_barrier_semaphore()
    for k in range(1, n):
        pl.semaphore_signal(barrier, inc=1, device_id={"dp": lax.rem(me + k, n)})
    pl.semaphore_signal(barrier, inc=1, device_id={"tensor": other})

    pending = []

    def send(src, dst, ssem, rsem, where):
        copy = pltpu.make_async_remote_copy(
            src_ref=src, dst_ref=dst, send_sem=ssem, recv_sem=rsem, device_id=where
        )
        copy.start()
        pending.append(copy)
        return copy

    load_po.wait()
    load_qg.wait()
    q_out = dot(qg_v[...].reshape(queries * q_length, -1), po_v[...], NT)
    load_pi.wait()
    load_qh.wait()
    load_tg = load(tg, tg_v, 8)
    load_th = []
    for s in range(seqs):
        for j in range(chunks):
            rows = pl.ds(j * chunk, chunk)
            copy = pltpu.make_async_copy(th.at[s, rows], th_v.at[s, rows], h_sem.at[s, j])
            copy.start()
            load_th.append(copy)

    q_in = dot(qh_v[...].reshape(queries * q_length, -1), pi_v[...], NT)
    q_both = jnp.concatenate([q_in, q_out], axis=1)
    first, second = q_both[:q_length], q_both[q_length:]
    q_send[...] = jnp.where(core == 0, second, first)
    q_mine[...] = jnp.where(core == 0, first, second)
    pl.semaphore_wait(barrier, n)
    ex_q = send(q_send, q_recv, ex_send, ex_recv, {"tensor": other})

    width = pi.shape[0]
    load_qp.wait()
    load_oi.wait()
    load_ii.wait()
    ex_q.wait_recv()
    total = q_mine[...] + q_recv[...]
    padding = jnp.where(core == 0, qp_s[0], qp_s[1])
    weights = token_weights(q_length, 0, q_length, padding)
    block = outer(total[:, width:] * weights, total[:, :width])
    conditioned = dot32(dot32(oi_v[...], block, NN), ii_v[...], NN)
    slot = me * queries + core
    gathered[slot] = pack(conditioned)
    ex_g = []
    for k in range(1, n):
        ex_g.append(
            send(gathered.at[slot], gathered.at[slot], g_ssem.at[k], g_rsem.at[k], {"dp": lax.rem(me + k, n)})
        )
    ex_f = [send(gathered.at[slot], gathered.at[slot], f_ssem.at[0], f_rsem.at[0], {"tensor": other})]

    def pass_on(k):
        ex_g[k - 1].wait_recv()
        source = lax.rem(me + (n - k), n) * queries + core
        ex_f.append(
            send(gathered.at[source], gathered.at[source], f_ssem.at[k], f_rsem.at[k], {"tensor": other})
        )

    load_tg.wait()
    ex_o = []
    for s in range(seqs):
        o_send[s] = pack(dot(tg_v[s], po_v[...], NT))
        ex_o.append(send(o_send.at[s], o_recv.at[s], o_ssem.at[s], o_rsem.at[s], {"tensor": other}))

    ex_i = []
    for copy in load_th:
        copy.wait()
    both = dot(th_v[...].reshape(seqs * length, -1), pi_v[...], NT)
    for s in range(seqs):
        for j in range(chunks):
            first_row = s * length + j * chunk
            i_send[s, j] = pack(both[first_row : first_row + chunk])
            ex_i.append(
                send(i_send.at[s, j], i_recv.at[s, j], i_ssem.at[s, j], i_rsem.at[s, j], {"tensor": other})
            )
    load_tp.wait()
    facing = []
    for s in range(seqs):
        ex_o[s].wait_recv()
        weights = token_weights(length, 0, length, tp_s[s])
        facing.append(unpack(o_send[s] + o_recv[s]) * weights)

    for k in range(1, n):
        pass_on(k)

    ones = jnp.ones((8, 2 * width), BF16)
    for s in range(seqs):
        block = jnp.zeros((width, width), F32)
        for j in range(chunks):
            ex_i[s * chunks + j].wait_recv()
            in_side = unpack(i_send[s, j] + i_recv[s, j])
            block += outer(facing[s][j * chunk : (j + 1) * chunk], in_side)
        if s == 0:
            for copy in ex_f:
                copy.wait_recv()
        sums = jnp.sum(gathered[...] * pack(block)[None], axis=1)
        high, low = halves(sums)
        out[pl.ds(s, 1), :] = (dot(ones, high, NT) + dot(ones, low, NT))[:1]

    for copy in pending:
        copy.wait_send()


def on_device(n, th, tg, tp, qh, qg, qp, pi, po, ii, oi):
    seqs, length, ff = th.shape
    queries, q_length, _ = qh.shape
    width = pi.shape[0]
    chunk = 256
    chunks = length // chunk
    dma = pltpu.SemaphoreType.DMA
    hbm = pl.BlockSpec(memory_space=pl.ANY)
    return pl.pallas_call(
        functools.partial(kernel, n, chunk),
        out_shape=jax.ShapeDtypeStruct((seqs, n * queries), F32),
        in_specs=[hbm] * 10,
        out_specs=pl.BlockSpec(memory_space=pltpu.VMEM),
        scratch_shapes=[
            pltpu.VMEM(th.shape, BF16),
            pltpu.VMEM(tg.shape, BF16),
            pltpu.SMEM(tp.shape, jnp.int32),
            pltpu.VMEM(qh.shape, BF16),
            pltpu.VMEM(qg.shape, BF16),
            pltpu.SMEM(qp.shape, jnp.int32),
            pltpu.VMEM(pi.shape, BF16),
            pltpu.VMEM(po.shape, BF16),
            pltpu.VMEM(ii.shape, F32),
            pltpu.VMEM(oi.shape, F32),
            pltpu.VMEM((q_length, 2 * width), F32),
            pltpu.VMEM((q_length, 2 * width), F32),
            pltpu.VMEM((q_length, 2 * width), F32),
            pltpu.VMEM((seqs, length // 2, 2 * width), F32),
            pltpu.VMEM((seqs, length // 2, 2 * width), F32),
            pltpu.VMEM((seqs, chunks, chunk // 2, 2 * width), F32),
            pltpu.VMEM((seqs, chunks, chunk // 2, 2 * width), F32),
            pltpu.VMEM((n * queries, width // 2, 2 * width), F32),
            dma((9,)),
            dma((seqs, chunks)),
            dma,
            dma,
            dma((seqs,)),
            dma((seqs,)),
            dma((seqs, chunks)),
            dma((seqs, chunks)),
            dma((n,)),
            dma((n,)),
            dma((n,)),
            dma((n,)),
        ],
        compiler_params=pltpu.CompilerParams(
            collective_id=0, has_side_effects=True, vmem_limit_bytes=56 * 1024 * 1024
        ),
        cost_estimate=pl.CostEstimate(
            flops=2 * width * (seqs * length + queries * q_length) * (ff + tg.shape[2]),
            bytes_accessed=2 * (seqs * length + queries * q_length) * (ff + tg.shape[2]),
            transcendentals=0,
        ),
    )(th, tg, tp, qh, qg, qp, pi, po, ii, oi)


def solution(mesh):
    rows = ("groups", "dp")
    in_specs = (
        P(rows, None, "tensor"),
        P(rows, None, "tensor"),
        P(rows),
        P(rows, None, "tensor"),
        P(rows, None, "tensor"),
        P(rows),
        P(None, "tensor"),
        P(None, "tensor"),
        P(),
        P(),
    )
    return jax.shard_map(
        functools.partial(on_device, mesh.shape["dp"]),
        mesh=mesh,
        in_specs=in_specs,
        out_specs=P(rows, None),
        check_vma=False,
    )
```

```python
import functools

import jax
import jax.numpy as jnp
from jax import lax
from jax.experimental import pallas as pl
from jax.experimental.pallas import tpu as pltpu
from jax.sharding import PartitionSpec as P

F32 = jnp.float32
BF16 = jnp.bfloat16
NT = (((1,), (1,)), ((), ()))
TN = (((0,), (0,)), ((), ()))
NN = (((1,), (0,)), ((), ()))


def dot(a, b, dims):
    return lax.dot_general(a, b, dims, preferred_element_type=F32)


def halves(x):
    high = x.astype(BF16)
    return high, (x - high.astype(F32)).astype(BF16)


def dot32(a, b, dims):
    a_high, a_low = halves(a)
    b_high, b_low = halves(b)
    return dot(a_high, b_high, dims) + (dot(a_high, b_low, dims) + dot(a_low, b_high, dims))


def outer(out_side, in_side):
    width = out_side.shape[1]
    left = jnp.concatenate(halves(out_side), axis=1)
    right = jnp.concatenate(halves(in_side), axis=1)
    full = dot(left, right, TN)
    return full[:width, :width] + (full[:width, width:] + full[width:, :width])


def pack(x):
    half = x.shape[0] // 2
    return jnp.concatenate([x[:half], x[half:]], axis=1)


def unpack(x):
    half = x.shape[1] // 2
    return jnp.concatenate([x[:, :half], x[:, half:]], axis=0)


def token_weights(tokens, first, length, padding):
    position = first + lax.broadcasted_iota(jnp.int32, (tokens, 1), 0)
    count = jnp.full((tokens, 1), length - padding, jnp.int32)
    return jnp.where(position < count, 1.0 / count.astype(F32), 0.0)


def kernel(
    n,
    chunk,
    th, tg, tp, qh, qg, qp, pi, po, ii, oi,
    out,
    th_v, tg_v, tp_s, qh_v, qg_v, qp_s, pi_v, po_v, ii_v, oi_v,
    q_mine, q_send, q_recv,
    o_send, o_recv, i_send, i_recv, gathered,
    load_sem, h_sem, ex_send, ex_recv, o_ssem, o_rsem, i_ssem, i_rsem,
    g_ssem, g_rsem, f_ssem, f_rsem,
):
    seqs, length, _ = th.shape
    queries, q_length, _ = qh.shape
    chunks = length // chunk
    me = lax.axis_index("dp")
    core = lax.axis_index("tensor")
    other = 1 - core

    def load(src, dst, k):
        copy = pltpu.make_async_copy(src, dst, load_sem.at[k])
        copy.start()
        return copy

    load_po = load(po, po_v, 0)
    load_qg = load(qg, qg_v, 1)
    load_pi = load(pi, pi_v, 2)
    load_qh = load(qh, qh_v, 3)
    load_qp = load(qp, qp_s, 4)
    load_tp = load(tp, tp_s, 5)
    load_oi = load(oi, oi_v, 6)
    load_ii = load(ii, ii_v, 7)
    barrier = pltpu.get_barrier_semaphore()
    for k in range(1, n):
        pl.semaphore_signal(barrier, inc=1, device_id={"dp": lax.rem(me + k, n)})
    pl.semaphore_signal(barrier, inc=1, device_id={"tensor": other})

    pending = []

    def send(src, dst, ssem, rsem, where):
        copy = pltpu.make_async_remote_copy(
            src_ref=src, dst_ref=dst, send_sem=ssem, recv_sem=rsem, device_id=where
        )
        copy.start()
        pending.append(copy)
        return copy

    load_po.wait()
    load_qg.wait()
    q_out = dot(qg_v[...].reshape(queries * q_length, -1), po_v[...], NT)
    load_pi.wait()
    load_qh.wait()
    load_tg = load(tg, tg_v, 8)
    load_th = [pltpu.make_async_copy(th, th_v, h_sem.at[0, 0])]
    load_th[0].start()
    q_in = dot(qh_v[...].reshape(queries * q_length, -1), pi_v[...], NT)
    q_both = jnp.concatenate([q_in, q_out], axis=1)
    first, second = q_both[:q_length], q_both[q_length:]
    q_send[...] = jnp.where(core == 0, second, first)
    q_mine[...] = jnp.where(core == 0, first, second)
    pl.semaphore_wait(barrier, n)
    ex_q = send(q_send, q_recv, ex_send, ex_recv, {"tensor": other})

    width = pi.shape[0]
    load_qp.wait()
    load_oi.wait()
    load_ii.wait()
    ex_q.wait_recv()
    total = q_mine[...] + q_recv[...]
    padding = jnp.where(core == 0, qp_s[0], qp_s[1])
    weights = token_weights(q_length, 0, q_length, padding)
    block = outer(total[:, width:] * weights, total[:, :width])
    conditioned = dot32(dot32(oi_v[...], block, NN), ii_v[...], NN)
    slot = me * queries + core
    gathered[slot] = pack(conditioned)
    ex_g = []
    for k in range(1, n):
        ex_g.append(
            send(gathered.at[slot], gathered.at[slot], g_ssem.at[k], g_rsem.at[k], {"dp": lax.rem(me + k, n)})
        )
    ex_f = [send(gathered.at[slot], gathered.at[slot], f_ssem.at[0], f_rsem.at[0], {"tensor": other})]

    def pass_on(k):
        ex_g[k - 1].wait_recv()
        source = lax.rem(me + (n - k), n) * queries + core
        ex_f.append(
            send(gathered.at[source], gathered.at[source], f_ssem.at[k], f_rsem.at[k], {"tensor": other})
        )

    load_tg.wait()
    ex_o = []
    both_out = dot(tg_v[...].reshape(seqs * length, -1), po_v[...], NT)
    for s in range(seqs):
        o_send[s] = pack(both_out[s * length : (s + 1) * length])
        ex_o.append(send(o_send.at[s], o_recv.at[s], o_ssem.at[s], o_rsem.at[s], {"tensor": other}))

    ex_i = []
    for copy in load_th:
        copy.wait()
    both = dot(th_v[...].reshape(seqs * length, -1), pi_v[...], NT)
    for s in range(seqs):
        for j in range(chunks):
            first_row = s * length + j * chunk
            i_send[s, j] = pack(both[first_row : first_row + chunk])
            ex_i.append(
                send(i_send.at[s, j], i_recv.at[s, j], i_ssem.at[s, j], i_rsem.at[s, j], {"tensor": other})
            )
    load_tp.wait()
    facing = []
    for s in range(seqs):
        ex_o[s].wait_recv()
        weights = token_weights(length, 0, length, tp_s[s])
        facing.append(unpack(o_send[s] + o_recv[s]) * weights)

    for k in range(1, n):
        pass_on(k)

    ones = jnp.ones((8, 2 * width), BF16)
    for s in range(seqs):
        block = jnp.zeros((width, width), F32)
        for j in range(chunks):
            ex_i[s * chunks + j].wait_recv()
            in_side = unpack(i_send[s, j] + i_recv[s, j])
            block += outer(facing[s][j * chunk : (j + 1) * chunk], in_side)
        if s == 0:
            for copy in ex_f:
                copy.wait_recv()
        sums = jnp.sum(gathered[...] * pack(block)[None], axis=1)
        high, low = halves(sums)
        out[pl.ds(s, 1), :] = (dot(ones, high, NT) + dot(ones, low, NT))[:1]

    for copy in pending:
        copy.wait_send()


def on_device(n, th, tg, tp, qh, qg, qp, pi, po, ii, oi):
    seqs, length, ff = th.shape
    queries, q_length, _ = qh.shape
    width = pi.shape[0]
    chunk = 256
    chunks = length // chunk
    dma = pltpu.SemaphoreType.DMA
    hbm = pl.BlockSpec(memory_space=pl.ANY)
    return pl.pallas_call(
        functools.partial(kernel, n, chunk),
        out_shape=jax.ShapeDtypeStruct((seqs, n * queries), F32),
        in_specs=[hbm] * 10,
        out_specs=pl.BlockSpec(memory_space=pltpu.VMEM),
        scratch_shapes=[
            pltpu.VMEM(th.shape, BF16),
            pltpu.VMEM(tg.shape, BF16),
            pltpu.SMEM(tp.shape, jnp.int32),
            pltpu.VMEM(qh.shape, BF16),
            pltpu.VMEM(qg.shape, BF16),
            pltpu.SMEM(qp.shape, jnp.int32),
            pltpu.VMEM(pi.shape, BF16),
            pltpu.VMEM(po.shape, BF16),
            pltpu.VMEM(ii.shape, F32),
            pltpu.VMEM(oi.shape, F32),
            pltpu.VMEM((q_length, 2 * width), F32),
            pltpu.VMEM((q_length, 2 * width), F32),
            pltpu.VMEM((q_length, 2 * width), F32),
            pltpu.VMEM((seqs, length // 2, 2 * width), F32),
            pltpu.VMEM((seqs, length // 2, 2 * width), F32),
            pltpu.VMEM((seqs, chunks, chunk // 2, 2 * width), F32),
            pltpu.VMEM((seqs, chunks, chunk // 2, 2 * width), F32),
            pltpu.VMEM((n * queries, width // 2, 2 * width), F32),
            dma((9,)),
            dma((seqs, chunks)),
            dma,
            dma,
            dma((seqs,)),
            dma((seqs,)),
            dma((seqs, chunks)),
            dma((seqs, chunks)),
            dma((n,)),
            dma((n,)),
            dma((n,)),
            dma((n,)),
        ],
        compiler_params=pltpu.CompilerParams(
            collective_id=0, has_side_effects=True, vmem_limit_bytes=56 * 1024 * 1024
        ),
        cost_estimate=pl.CostEstimate(
            flops=2 * width * (seqs * length + queries * q_length) * (ff + tg.shape[2]),
            bytes_accessed=2 * (seqs * length + queries * q_length) * (ff + tg.shape[2]),
            transcendentals=0,
        ),
    )(th, tg, tp, qh, qg, qp, pi, po, ii, oi)


def solution(mesh):
    rows = ("groups", "dp")
    in_specs = (
        P(rows, None, "tensor"),
        P(rows, None, "tensor"),
        P(rows),
        P(rows, None, "tensor"),
        P(rows, None, "tensor"),
        P(rows),
        P(None, "tensor"),
        P(None, "tensor"),
        P(),
        P(),
    )
    return jax.shard_map(
        functools.partial(on_device, mesh.shape["dp"]),
        mesh=mesh,
        in_specs=in_specs,
        out_specs=P(rows, None),
        check_vma=False,
    )
```
